32 devices in a mesh: ep: 8 (over z, x), tp: 4 (over y, core).
Axes of the slice: x: 2, y: 2, z: 4, core: 2. Of those that a mesh axis runs over, the one named last changes fastest.
Arguments:
- tokens: bfloat16 [4096, 1024], P('ep'), may hold values from -6 to 6
- norm_attn: float32 [1024], replicated, may hold values from 0.1 to 1.9
- w_query: bfloat16 [1024, 1024], P(None, 'tp'), may hold values from -0.1875 to 0.1875
- w_key: bfloat16 [1024, 512], P(None, 'tp'), may hold values from -0.1875 to 0.1875
- w_value: bfloat16 [1024, 512], P(None, 'tp'), may hold values from -0.1875 to 0.1875
- w_out: bfloat16 [1024, 1024], P('tp'), may hold values from -2 to 2
- norm_moe: float32 [1024], replicated, may hold values from 0.1 to 1.9
- router: bfloat16 [1024, 32], replicated, may hold values from -0.09375 to 0.09375
- expert_gate: bfloat16 [32, 1024, 512], P('ep', None, 'tp'), may hold values from -0.1875 to 0.1875
- expert_up: bfloat16 [32, 1024, 512], P('ep', None, 'tp'), may hold values from -0.1875 to 0.1875
- expert_down: bfloat16 [32, 512, 1024], P('ep', 'tp'), may hold values from -1 to 1
- lengths: int32 [8, 4], P('ep'), may hold values from 1 to 256, 512 in all within a row
- expert_ids: int32 [4096, 8], P('ep'), may hold values from 0 to 31, all different within a row; in each aligned block of 512 rows (0 to 511, 512 to 1023, ...) at most 192 rows name the same one
- out_grad: bfloat16 [4096, 1024], P('ep'), may hold values from -6 to 6
Outputs:
- output: bfloat16 [4096, 1024], P('ep')
- grad_tokens: bfloat16 [4096, 1024], P('ep')
- grad_norm_attn: float32 [1024], replicated
- grad_w_query: float32 [1024, 1024], P(None, 'tp')
- grad_w_key: float32 [1024, 512], P(None, 'tp')
- grad_w_value: float32 [1024, 512], P(None, 'tp')
- grad_w_out: float32 [1024, 1024], P('tp')
- grad_norm_moe: float32 [1024], replicated
- grad_router: float32 [1024, 32], replicated
- grad_expert_gate: float32 [32, 1024, 512], P('ep', None, 'tp')
- grad_expert_up: float32 [32, 1024, 512], P('ep', None, 'tp')
- grad_expert_down: float32 [32, 512, 1024], P('ep', 'tp')
The draws below stay inside these ranges and needn't reach their ends.
Inputs may be any that keep to these rules, and one draw needn't show every extreme that they name: Each group's 4 lengths sum to 512; in every group the longest is exactly 256. `expert_ids`: each token names 8 different experts. Among the 512 tokens of one group no expert is named more than 192 times, a bound that some block reaches.
All inputs are finite; a program needn't handle non-finite values.
Results may differ from the reference program's by a relative error of at most 0.02.
Values may be sent and summed in bfloat16 or wider, within the bound.
A program may use at most 256 MiB of HBM per device.

```python
import math
import jax
import jax.numpy as jnp
import numpy as np
from jax import lax

D = 1024
Q_HEADS = 16
KV_HEADS = 8
HEAD = 64
FF = 512
EXPERTS = 32
TOP = 8
TOK_GRP = 512
SEQS = 4
SEQ_MAX = 256
CAP = 192
TOKENS = 4096
N_EP = 8


def steps_of(key, extent, pieces, low, high):
    level = 1.0
    for axis_at, shards_of in pieces:
        draws = jax.random.uniform(jax.random.fold_in(jax.random.fold_in(key, 6), axis_at), (shards_of,), jnp.float32, low / len(pieces), high / len(pieces))
        level = level * jnp.repeat(jnp.exp(draws), extent[axis_at] // shards_of).reshape((-1,) + (1,) * (len(extent) - 1 - axis_at))
    return level


def profile(number_of, total, most, slope):
    weights = [(1 << 20) // math.isqrt(standing ** slope) + 1 for standing in range(2, number_of + 1)]
    surplus, counts = total - most - (number_of - 1), [1] * (number_of - 1)
    while surplus > 0:
        free = [i for i in range(number_of - 1) if counts[i] < most]
        mass, budget = sum([weights[i] for i in free]), surplus
        for i in free:
            addition = min(most - counts[i], max(1, budget * weights[i] // mass), surplus)
            counts[i] = counts[i] + addition
            surplus = surplus - addition
    return np.array([most] + counts)


def uneven(key, number_of, total, bound, lean):
    if number_of == 2:
        one = jax.random.randint(key, (), max(1, total - bound), min(bound, total - 1) + 1)
        return jnp.stack([one, total - one])
    tallies = jnp.asarray(profile(number_of, total, bound, lean), jnp.int32)
    pairs = (number_of - 1) // 2
    giver, sink = tallies[1:1 + 2 * pairs:2], tallies[2:2 + 2 * pairs:2]
    margin = jnp.minimum(giver - 1, bound - sink)
    passed = jax.random.randint(jax.random.fold_in(key, 1), (pairs,), 0, 1 << 20) % (margin + 1)
    tallies = tallies.at[1:1 + 2 * pairs:2].set(giver - passed).at[2:2 + 2 * pairs:2].set(sink + passed)
    return tallies[jax.random.permutation(jax.random.fold_in(key, 2), number_of)]


def assign_block(rng, own, number, rows, amount, top, reach, skew):
    ranking = jax.random.permutation(rng, amount)
    packed, usual = portions_of(amount, rows * top, reach, skew, True), portions_of(amount, rows * top, reach, skew, False)
    places = jnp.arange(amount)

    def named(sizes, rotation):
        used = int((sizes > 0).sum())
        fixed = max(1, used // 4)
        shifted = fixed + (places - fixed + rotation * (used - fixed)) % max(1, amount - fixed)
        return jnp.zeros((amount,), jnp.int32).at[ranking[jnp.where(places < fixed, places, shifted)]].set(jnp.asarray(sizes, jnp.int32))

    sizes = jnp.where(number % 4 == 0, named(packed, number // 4), named(usual, number - number // 4 - 1))
    mixed = jax.random.permutation(jax.random.fold_in(own, 3), amount)
    source_of, taker = mixed[0:amount // 2 * 2:2], mixed[1:amount // 2 * 2:2]
    room = jnp.minimum(sizes[source_of] - 1, reach - sizes[taker]) // 2
    room = jnp.where((source_of == ranking[0]) | (taker == ranking[0]) | (sizes[taker] == 0), 0, jnp.maximum(room, 0))
    shifted = jax.random.randint(jax.random.fold_in(own, 4), (amount // 2,), 0, 1 << 20) % (room + 1)
    sizes = sizes.at[source_of].add(-shifted).at[taker].add(shifted)
    labels = jnp.searchsorted(jnp.cumsum(sizes), jnp.arange(rows * top), side="right").astype(jnp.int32)
    table = labels.reshape(top, rows).T
    table = table[jax.random.permutation(jax.random.fold_in(own, 1), rows)]
    rotation = jax.random.randint(jax.random.fold_in(own, 2), (rows, 1), 0, top)
    return jnp.take_along_axis(table, (jnp.arange(top)[None, :] + rotation) % top, axis=1)


def portions_of(count, total, bound, lean, full):
    weights = [(1 << 20) // math.isqrt(standing ** lean) + 1 for standing in range(1, count + 1)]
    largest = bound if full else min(bound, max(-(-total // count), total * weights[0] // sum(weights)))
    least = 1 if total - largest >= count - 1 else 0
    counts, spare = [largest] + [least] * (count - 1), total - largest - least * (count - 1)
    while spare > 0:
        movable = [i for i in range(1, count) if counts[i] < largest] or [i for i in range(1, count) if counts[i] < bound]
        whole, budget = sum([weights[i] for i in movable]), spare
        for i in movable:
            addition = min(bound - counts[i], max(1, budget * weights[i] // whole), spare)
            counts[i] = counts[i] + addition
            spare = spare - addition
    return np.array(counts)


def normal_values(key, extent, scale, most, split=(), held_as=jnp.bfloat16):
    values = jax.random.normal(key, extent, jnp.float32) * scale
    if len(split) > 0:
        values = steps_of(key, extent, split, -0.22, 0.18) * values
    return jnp.clip(values, min=-most, max=most).astype(held_as)


def setup_inputs(seed: int = 0) -> dict:
    seeds = jax.random.split(jax.random.key(seed), 15)
    tokens = normal_values(seeds[0], (TOKENS, D), 1.0, 6.0, ((0, 8),))
    norm_attn = jnp.clip(1.0 + 0.18 * jax.random.normal(seeds[1], (D,), jnp.float32), 0.1, 1.9)
    w_query = normal_values(seeds[2], (D, Q_HEADS * HEAD), D ** -0.5, 0.1875, ((1, 4),))
    w_key = normal_values(seeds[3], (D, KV_HEADS * HEAD), D ** -0.5, 0.1875, ((1, 4),))
    w_value = normal_values(seeds[4], (D, KV_HEADS * HEAD), D ** -0.5, 0.1875, ((1, 4),))
    w_out = normal_values(seeds[5], (Q_HEADS * HEAD, D), 8 ** -0.5, 2.0, ((0, 4),))
    norm_moe = jnp.clip(1.0 + 0.18 * jax.random.normal(seeds[6], (D,), jnp.float32), 0.1, 1.9)
    router = normal_values(seeds[7], (D, EXPERTS), (4 * D) ** -0.5, 0.09375)
    expert_gate = normal_values(seeds[8], (EXPERTS, D, FF), D ** -0.5, 0.1875, ((0, 8), (2, 4)))
    expert_up = normal_values(seeds[9], (EXPERTS, D, FF), D ** -0.5, 0.1875, ((0, 8), (2, 4)))
    expert_down = normal_values(seeds[10], (EXPERTS, FF, D), (FF // 16) ** -0.5, 1.0, ((0, 8), (1, 4)))
    lengths = jax.vmap(lambda own: uneven(own, SEQS, TOK_GRP, SEQ_MAX, 2))(jax.random.split(seeds[11], N_EP)).reshape((N_EP, SEQS)).astype(jnp.int32)
    expert_ids_keys = jax.random.split(jax.random.fold_in(seeds[12], 1), TOKENS // TOK_GRP)
    expert_ids_turns = jax.random.permutation(jax.random.fold_in(seeds[12], 3), TOKENS // TOK_GRP)
    expert_ids = jax.vmap(lambda own, number: assign_block(jax.random.fold_in(seeds[12], 2), own, number, TOK_GRP, EXPERTS, TOP, CAP, 1))(expert_ids_keys, expert_ids_turns).reshape((TOKENS, TOP))
    out_grad = normal_values(seeds[13], (TOKENS, D), 1.0, 6.0, ((0, 8),))
    return dict(tokens=tokens, norm_attn=norm_attn, w_query=w_query, w_key=w_key, w_value=w_value, w_out=w_out, norm_moe=norm_moe, router=router, expert_gate=expert_gate, expert_up=expert_up, expert_down=expert_down, lengths=lengths, expert_ids=expert_ids, out_grad=out_grad)


EPSILON = 1e-06
ROPE_BASE = 10000.0

@jax.custom_vjp
def low(v):
    return lax.optimization_barrier(v.astype(jnp.bfloat16)).astype(jnp.float32)

@jax.custom_vjp
def low_back(v):
    return v

def low_keep(v):
    return (low(v), None)

def low_pass(kept, grad):
    return (grad,)

def back_keep(v):
    return (v, None)

def back_low(kept, grad):
    return (low(grad),)
low.defvjp(low_keep, low_pass)
low_back.defvjp(back_keep, back_low)

def seq_layout(seq_lengths, tok_rows):
    seq_ends = jnp.cumsum(seq_lengths, dtype=jnp.int32)
    seq_starts = seq_ends - seq_lengths
    places = jnp.arange(tok_rows, dtype=jnp.int32)
    segment = lax.optimization_barrier(jnp.sum((places[:, None] >= seq_ends[None, :]).astype(jnp.int32), axis=1, dtype=jnp.int32))
    slot_match = segment[:, None] == jnp.arange(seq_lengths.shape[0], dtype=jnp.int32)[None, :]
    begins = lax.optimization_barrier(jnp.sum(jnp.where(slot_match, seq_starts[None, :], 0), axis=1, dtype=jnp.int32))
    return (segment, places - begins)

def rope_tables(position, head_size):
    half_width = head_size // 2
    inverse = ROPE_BASE ** (-2.0 * jnp.arange(half_width, dtype=jnp.float32) / head_size)
    angles = position.astype(jnp.float32)[:, None] * inverse[None, :]
    angles = jnp.concatenate([angles, angles], axis=1)
    return (jnp.cos(angles), jnp.sin(angles))

def rotate(values, cosine, sine_part):
    half_width = values.shape[-1] // 2
    turned = jnp.concatenate([-values[..., half_width:], values[..., :half_width]], axis=-1)
    return values * cosine[:, None, :] + turned * sine_part[:, None, :]

def slot_table(expert_ids, expert_count, capacity):
    flat_ids = expert_ids.reshape(-1)
    pair_count = flat_ids.shape[0]
    one_hot = (flat_ids[:, None] == jnp.arange(expert_count, dtype=jnp.int32)[None, :]).astype(jnp.int32)
    earlier = jnp.cumsum(one_hot, axis=0, dtype=jnp.int32) - one_hot
    ranks = lax.optimization_barrier(jnp.sum(earlier * one_hot, axis=1, dtype=jnp.int32))
    pair_slot = flat_ids * capacity + ranks
    slot_owner = jnp.full((expert_count * capacity,), pair_count, jnp.int32).at[pair_slot].set(jnp.arange(pair_count, dtype=jnp.int32))
    return (pair_slot, slot_owner)

def layer(params, x_group, seq_lengths, group_ids):
    norm_attn, w_query, w_key, w_value, w_out, norm_moe, router, expert_gate, expert_up, expert_down = params
    highest = lax.Precision.HIGHEST
    tok_rows = x_group.shape[0]
    group_size = Q_HEADS // KV_HEADS
    scale_one = lax.rsqrt(lax.optimization_barrier(jnp.mean(x_group * x_group, axis=1, keepdims=True)) + EPSILON)
    normed_one = low(x_group * scale_one * norm_attn)
    query_raw = low_back(jnp.dot(normed_one, w_query, precision=highest)).reshape(tok_rows, Q_HEADS, HEAD)
    key_raw = low_back(jnp.dot(normed_one, w_key, precision=highest)).reshape(tok_rows, KV_HEADS, HEAD)
    value_low = low(low_back(jnp.dot(normed_one, w_value, precision=highest))).reshape(tok_rows, KV_HEADS, HEAD)
    segment, position = seq_layout(seq_lengths, tok_rows)
    cosine, sine_part = rope_tables(position, HEAD)
    query_rot = low(rotate(query_raw, cosine, sine_part)).reshape(tok_rows, KV_HEADS, group_size, HEAD)
    key_rot = low(rotate(key_raw, cosine, sine_part))
    block_rows = min(512, tok_rows)
    score_scale = HEAD ** (-0.5)
    key_place = jnp.arange(tok_rows, dtype=jnp.int32)

    def one_block(block_index):
        first_row = block_index * block_rows
        query_block = lax.dynamic_slice_in_dim(query_rot, first_row, block_rows, 0)
        row_place = first_row + jnp.arange(block_rows, dtype=jnp.int32)
        row_segment = lax.dynamic_slice_in_dim(segment, first_row, block_rows, 0)
        allowed = (row_segment[:, None] == segment[None, :]) & (key_place[None, :] <= row_place[:, None])
        scores = low_back(jnp.einsum('bkgh,nkh->kgbn', query_block, key_rot, precision=highest) * score_scale)
        scores = jnp.where(allowed, scores, -1e+30)
        row_max = lax.optimization_barrier(jnp.max(scores, axis=-1, keepdims=True))
        exp_terms = jnp.exp(scores - row_max)
        probs = low(exp_terms / lax.optimization_barrier(jnp.sum(exp_terms, axis=-1, keepdims=True)))
        return jnp.einsum('kgbn,nkh->bkgh', probs, value_low, precision=highest)
    mixed_out = lax.map(jax.checkpoint(one_block), jnp.arange(tok_rows // block_rows, dtype=jnp.int32))
    attended = low_back(low(mixed_out.reshape(tok_rows, Q_HEADS * HEAD)))
    residual = x_group + low_back(jnp.dot(attended, w_out, precision=highest))
    scale_two = lax.rsqrt(lax.optimization_barrier(jnp.mean(residual * residual, axis=1, keepdims=True)) + EPSILON)
    normed_two = low(residual * scale_two * norm_moe)
    logits = jnp.dot(normed_two, router, precision=highest)
    chosen = jnp.take_along_axis(logits, group_ids, axis=1)
    chosen_exp = jnp.exp(chosen - lax.optimization_barrier(jnp.max(chosen, axis=1, keepdims=True)))
    gates = chosen_exp / lax.optimization_barrier(jnp.sum(chosen_exp, axis=1, keepdims=True))
    pair_slot, slot_owner = slot_table(group_ids, EXPERTS, CAP)
    padded_two = jnp.concatenate([normed_two, jnp.zeros((1, D), jnp.float32)], axis=0)
    expert_rows = low_back(padded_two[slot_owner // TOP].reshape(EXPERTS, CAP, D))
    gate_pre = low_back(jnp.einsum('ecd,edf->ecf', expert_rows, expert_gate, precision=highest))
    up_pre = low_back(jnp.einsum('ecd,edf->ecf', expert_rows, expert_up, precision=highest))
    active = low(gate_pre * jax.nn.sigmoid(gate_pre) * up_pre)
    expert_out = low_back(low(jnp.einsum('ecf,efd->ecd', active, expert_down, precision=highest)))
    per_pair = expert_out.reshape(EXPERTS * CAP, D)[pair_slot].reshape(tok_rows, TOP, D)
    mixture = lax.optimization_barrier(jnp.sum(gates[:, :, None] * per_pair, axis=1))
    return residual + mixture

def reference(tokens, norm_attn, w_query, w_key, w_value, w_out, norm_moe, router, expert_gate, expert_up, expert_down, lengths, expert_ids, out_grad):
    params = tuple((weight.astype(jnp.float32) for weight in (norm_attn, w_query, w_key, w_value, w_out, norm_moe, router, expert_gate, expert_up, expert_down)))
    x_all = tokens.astype(jnp.float32).reshape(N_EP, TOK_GRP, D)
    ids_all = expert_ids.reshape(N_EP, TOK_GRP, TOP)
    grad_all = out_grad.astype(jnp.float32).reshape(N_EP, TOK_GRP, D)

    def accumulate(running, inputs):
        x_group, seq_lengths, group_ids, grad_group = inputs
        finals, pull = jax.vjp(lambda weights, values: layer(weights, values, seq_lengths, group_ids), params, x_group)
        grad_params, grad_input = pull(grad_group)
        running = jax.tree.map(lambda first, second: first + second, running, grad_params)
        return (running, (finals, grad_input))
    zeros_start = jax.tree.map(jnp.zeros_like, params)
    sums, (finals, grad_inputs) = lax.scan(accumulate, zeros_start, (x_all, lengths, ids_all, grad_all))
    output = finals.reshape(TOKENS, D).astype(jnp.bfloat16)
    grad_tokens = grad_inputs.reshape(TOKENS, D).astype(jnp.bfloat16)
    return (output, grad_tokens, sums[0], sums[1], sums[2], sums[3], sums[4], sums[5], sums[6], sums[7], sums[8], sums[9])
```

```python
import jax
import jax.numpy as jnp
import numpy as np
from jax import lax
from jax.sharding import PartitionSpec as P

HEAD = 64
EPSILON = 1e-06
ROPE_BASE = 10000.0
BOTH = ("ep", "tp")
BF = jnp.bfloat16
F32 = jnp.float32


def mm(a, b):
    return jnp.dot(a, b, preferred_element_type=F32)


def mm_nt(a, b):
    return lax.dot_general(a, b, (((1,), (1,)), ((), ())), preferred_element_type=F32)


def mm_tn(a, b):
    return lax.dot_general(a, b, (((0,), (0,)), ((), ())), preferred_element_type=F32)


def seq_layout(seq_lengths, tok_rows):
    seq_ends = jnp.cumsum(seq_lengths, dtype=jnp.int32)
    seq_starts = seq_ends - seq_lengths
    places = jnp.arange(tok_rows, dtype=jnp.int32)
    segment = jnp.sum(
        (places[:, None] >= seq_ends[None, :]).astype(jnp.int32), axis=1, dtype=jnp.int32
    )
    slot_match = segment[:, None] == jnp.arange(seq_lengths.shape[0], dtype=jnp.int32)[None, :]
    begins = jnp.sum(jnp.where(slot_match, seq_starts[None, :], 0), axis=1, dtype=jnp.int32)
    return (segment, places - begins)


def turn_columns(weights):
    rows, columns = weights.shape
    split = weights.reshape(rows, columns // HEAD, 2, HEAD // 2)
    return jnp.stack([-split[:, :, 1], split[:, :, 0]], axis=2).reshape(rows, columns)


def turn_matrix(columns):
    half = HEAD // 2
    turn = np.zeros((columns, columns), np.float32)
    for first in range(0, columns, HEAD):
        for i in range(half):
            turn[first + half + i, first + i] = 1.0
            turn[first + i, first + half + i] = -1.0
    return jnp.asarray(turn, BF)


def body(
    tokens,
    norm_attn,
    w_query,
    w_key,
    w_value,
    w_out,
    norm_moe,
    router,
    expert_gate,
    expert_up,
    expert_down,
    lengths,
    expert_ids,
    out_grad,
):
    highest = lax.Precision.HIGHEST
    tok_rows, width = tokens.shape
    q_cols, k_cols = w_query.shape[1], w_key.shape[1]
    kv = k_cols // HEAD
    group = q_cols // k_cols
    tp_size = lax.axis_size("tp")
    tp_at = lax.axis_index("tp")
    ep_at = lax.axis_index("ep")
    own = tok_rows // tp_size
    local_experts, _, ff = expert_gate.shape
    experts = router.shape[1]
    first = tp_at * own
    score_scale = HEAD ** (-0.5)

    def mine(array):
        return lax.dynamic_slice_in_dim(array, first, own, 0)

    grad_own = mine(out_grad)
    grad_all = lax.all_gather(grad_own, BOTH, axis=0, tiled=True)
    ids_own = mine(expert_ids)
    mask_own = jnp.sum(
        (ids_own[:, :, None] == jnp.arange(experts, dtype=jnp.int32)[None, None, :]).astype(F32),
        axis=1,
    )
    mask_all = lax.all_gather(mask_own.astype(BF), BOTH, axis=0, tiled=True)

    w_gate_up = jnp.concatenate(
        [
            jnp.transpose(expert_gate, (1, 0, 2)).reshape(width, local_experts * ff),
            jnp.transpose(expert_up, (1, 0, 2)).reshape(width, local_experts * ff),
        ],
        axis=1,
    )
    w_down = expert_down.reshape(local_experts * ff, width)

    x_full = tokens.astype(F32)
    scale_one = lax.rsqrt(jnp.mean(x_full * x_full, axis=1, keepdims=True) + EPSILON)
    normed_one = (x_full * scale_one * norm_attn).astype(BF)
    segment, position = seq_layout(lengths[0], tok_rows)
    half = HEAD // 2
    inverse = ROPE_BASE ** (-2.0 * jnp.arange(half, dtype=F32) / HEAD)
    angles = position.astype(F32)[:, None] * inverse[None, :]
    cos_half, sin_half = jnp.cos(angles), jnp.sin(angles)
    cosine = jnp.concatenate([cos_half, cos_half] * (q_cols // HEAD), axis=1)
    sine = jnp.concatenate([sin_half, sin_half] * (q_cols // HEAD), axis=1)
    w_all = jnp.concatenate(
        [w_query, turn_columns(w_query), w_key, turn_columns(w_key), w_value], axis=1
    )
    projected = mm(normed_one, w_all)
    at = 2 * q_cols
    query_low = (projected[:, :q_cols] * cosine + projected[:, q_cols:at] * sine).astype(BF)
    key_low = (
        projected[:, at : at + k_cols] * cosine[:, :k_cols]
        + projected[:, at + k_cols : at + 2 * k_cols] * sine[:, :k_cols]
    ).astype(BF)
    value_flat = projected[:, at + 2 * k_cols :].astype(BF)

    def heads_q(array):
        return (
            array.reshape(tok_rows, kv, group, HEAD)
            .transpose(1, 2, 0, 3)
            .reshape(kv, group * tok_rows, HEAD)
        )

    def flat_q(array):
        return (
            array.reshape(kv, group, tok_rows, HEAD)
            .transpose(2, 0, 1, 3)
            .reshape(tok_rows, q_cols)
        )

    def heads_k(array):
        return array.reshape(tok_rows, kv, HEAD).transpose(1, 0, 2)

    def flat_k(array):
        return array.transpose(1, 0, 2).reshape(tok_rows, k_cols)

    query, key, value = heads_q(query_low), heads_k(key_low), heads_k(value_flat)
    place = jnp.arange(tok_rows, dtype=jnp.int32)
    allowed = (segment[:, None] == segment[None, :]) & (place[None, :] <= place[:, None])
    allowed = jnp.concatenate([allowed] * group, axis=0)
    scores = jnp.einsum("kbh,knh->kbn", query, key, preferred_element_type=F32) * score_scale
    scores = jnp.where(allowed[None], scores, -1e30)
    row_max = jnp.max(scores, axis=-1, keepdims=True)
    exp_terms = jnp.exp(scores - row_max)
    probs_full = exp_terms / jnp.sum(exp_terms, axis=-1, keepdims=True)
    prob_low = probs_full.astype(BF)
    mixed = jnp.einsum("kbn,knh->kbh", prob_low, value, preferred_element_type=F32)
    attended = flat_q(mixed.astype(BF))
    attn_partial = mm(attended, w_out)
    x_own = mine(tokens).astype(F32)
    residual = x_own + lax.psum_scatter(attn_partial, "tp", scatter_dimension=0, tiled=True)
    scale_two = lax.rsqrt(jnp.mean(residual * residual, axis=1, keepdims=True) + EPSILON)
    normed_two = (residual * scale_two * norm_moe).astype(BF)

    rows_all = lax.all_gather(normed_two, BOTH, axis=0, tiled=True)
    logits = mm(rows_all, router)
    mask = mask_all > 0
    masked = jnp.where(mask, logits, -jnp.inf)
    chosen_exp = jnp.where(
        mask, jnp.exp(logits - jnp.max(masked, axis=1, keepdims=True)), 0.0
    )
    gates_all = chosen_exp / jnp.sum(chosen_exp, axis=1, keepdims=True)
    gates = lax.dynamic_slice_in_dim(gates_all, ep_at * local_experts, local_experts, 1)
    all_rows = rows_all.shape[0]
    wide = local_experts * ff
    gate_wide = jnp.concatenate(
        [jnp.broadcast_to(gates[:, e : e + 1], (all_rows, ff)) for e in range(local_experts)],
        axis=1,
    )
    pre = mm(rows_all, w_gate_up)
    gate_pre, up_pre = pre[:, :wide], pre[:, wide:]
    grad_act = mm_nt(grad_all, w_down)
    sig = jax.nn.sigmoid(gate_pre)
    active = gate_pre * sig * up_pre
    grad_gates_wide = active * grad_act
    grad_gates_part = jnp.concatenate(
        [
            jnp.sum(grad_gates_wide[:, e * ff : (e + 1) * ff], axis=1, keepdims=True)
            for e in range(local_experts)
        ],
        axis=1,
    )
    weighted = (gate_wide * active).astype(BF)
    scaled_grad = gate_wide * grad_act
    grad_pre = jnp.concatenate(
        [
            (scaled_grad * up_pre * sig * (1.0 + gate_pre * (1.0 - sig))).astype(BF),
            (scaled_grad * gate_pre * sig).astype(BF),
        ],
        axis=1,
    )
    gates_dense = lax.dynamic_update_slice_in_dim(
        jnp.zeros((all_rows, experts), F32), grad_gates_part, ep_at * local_experts, 1
    )
    grad_gates = lax.psum_scatter(gates_dense, BOTH, scatter_dimension=0, tiled=True)
    row_part = mm_nt(grad_pre, w_gate_up).astype(BF)
    row_grads = lax.psum_scatter(row_part, BOTH, scatter_dimension=0, tiled=True)
    mix_part = mm(weighted, w_down).astype(BF)
    mixture = lax.psum_scatter(mix_part, BOTH, scatter_dimension=0, tiled=True)
    grad_w_gu = mm_tn(rows_all, grad_pre)
    grad_w_gu = grad_w_gu.reshape(width, 2, local_experts, ff)
    grad_expert_gate = grad_w_gu[:, 0].transpose(1, 0, 2)
    grad_expert_up = grad_w_gu[:, 1].transpose(1, 0, 2)
    grad_expert_down = mm_tn(weighted, grad_all).reshape(local_experts, ff, width)

    output_own = (residual + mixture.astype(F32)).astype(BF)
    output = lax.all_gather(output_own, "tp", axis=0, tiled=True)
    logits_own = mm(normed_two, router)
    keep = mask_own > 0
    own_exp = jnp.where(
        keep,
        jnp.exp(logits_own - jnp.max(jnp.where(keep, logits_own, -jnp.inf), axis=1, keepdims=True)),
        0.0,
    )
    gates_own = own_exp / jnp.sum(own_exp, axis=1, keepdims=True)
    grad_logits = gates_own * (
        grad_gates - jnp.sum(gates_own * grad_gates, axis=1, keepdims=True)
    )
    grad_router_part = jnp.dot(grad_logits.T, normed_two.astype(F32), precision=highest)
    router_input = jnp.dot(grad_logits, router.astype(F32).T, precision=highest)
    grad_normed_two = row_grads.astype(F32) + router_input
    weighted_two = grad_normed_two * norm_moe
    grad_norm_moe = jnp.sum(grad_normed_two * residual * scale_two, axis=0)
    grad_residual = (
        grad_own.astype(F32)
        + scale_two * weighted_two
        - residual * scale_two**3 * jnp.mean(weighted_two * residual, axis=1, keepdims=True)
    )
    grad_attn = lax.all_gather(grad_residual.astype(BF), "tp", axis=0, tiled=True)
    grad_w_out = mm_tn(attended, grad_attn)

    grad_attended = heads_q(mm_nt(grad_attn, w_out).astype(BF))
    grad_prob = jnp.einsum("kbh,knh->kbn", grad_attended, value, preferred_element_type=F32)
    row_inner = jnp.sum(probs_full * grad_prob, axis=-1, keepdims=True)
    grad_scores = (probs_full * (grad_prob - row_inner)).astype(BF)
    grad_q = flat_q(jnp.einsum("kbn,knh->kbh", grad_scores, key, preferred_element_type=F32))
    grad_k = flat_k(jnp.einsum("kbn,kbh->knh", grad_scores, query, preferred_element_type=F32))
    grad_v = flat_k(jnp.einsum("kbn,kbh->knh", prob_low, grad_attended, preferred_element_type=F32))
    grad_q = grad_q * score_scale
    grad_k = grad_k * score_scale
    turn = turn_matrix(q_cols)
    grad_q_low = (grad_q * cosine + mm((grad_q * sine).astype(BF), turn)).astype(BF)
    grad_k_low = (
        grad_k * cosine[:, :k_cols]
        + mm((grad_k * sine[:, :k_cols]).astype(BF), turn[:k_cols, :k_cols])
    ).astype(BF)
    grad_qkv = jnp.concatenate([grad_q_low, grad_k_low, grad_v.astype(BF)], axis=1)
    w_qkv = jnp.concatenate([w_query, w_key, w_value], axis=1)
    input_part = mm_nt(grad_qkv, w_qkv)
    grad_normed_one = lax.psum_scatter(
        input_part.astype(BF), "tp", scatter_dimension=0, tiled=True
    ).astype(F32)
    scale_own = mine(scale_one)
    weighted_one = grad_normed_one * norm_attn
    grad_norm_attn = jnp.sum(input_part * x_full * scale_one, axis=0)
    tokens_own = (
        grad_residual
        + scale_own * weighted_one
        - x_own * scale_own**3 * jnp.mean(weighted_one * x_own, axis=1, keepdims=True)
    )
    grad_tokens = lax.all_gather(tokens_own.astype(BF), "tp", axis=0, tiled=True)
    small = jnp.concatenate([grad_router_part, grad_norm_moe[None]], axis=0)
    small = lax.psum(small, BOTH)
    grad_norm_attn = lax.psum(grad_norm_attn, BOTH)
    grad_w_out = lax.psum(grad_w_out.astype(BF), "ep").astype(F32)
    grad_w_qkv = lax.psum(mm_tn(normed_one, grad_qkv).astype(BF), "ep").astype(F32)
    return (
        output,
        grad_tokens,
        grad_norm_attn,
        grad_w_qkv[:, :q_cols],
        grad_w_qkv[:, q_cols : q_cols + k_cols],
        grad_w_qkv[:, q_cols + k_cols :],
        grad_w_out,
        small[experts],
        small[:experts].T,
        grad_expert_gate,
        grad_expert_up,
        grad_expert_down,
    )


def solution(mesh):
    in_specs = (
        P("ep", None),
        P(),
        P(None, "tp"),
        P(None, "tp"),
        P(None, "tp"),
        P("tp", None),
        P(),
        P(),
        P("ep", None, "tp"),
        P("ep", None, "tp"),
        P("ep", "tp", None),
        P("ep", None),
        P("ep", None),
        P("ep", None),
    )
    out_specs = (
        P("ep", None),
        P("ep", None),
        P(),
        P(None, "tp"),
        P(None, "tp"),
        P(None, "tp"),
        P("tp", None),
        P(),
        P(),
        P("ep", None, "tp"),
        P("ep", None, "tp"),
        P("ep", "tp", None),
    )
    return jax.shard_map(body, mesh=mesh, in_specs=in_specs, out_specs=out_specs, check_vma=False)
```

```python
import jax
import jax.numpy as jnp
import numpy as np
from jax import lax
from jax.sharding import PartitionSpec as P

HEAD = 64
EPSILON = 1e-06
ROPE_BASE = 10000.0
BOTH = ("tp", "ep")
BF = jnp.bfloat16
F32 = jnp.float32


def mm(a, b):
    return jnp.dot(a, b, preferred_element_type=F32)


def mm_nt(a, b):
    return lax.dot_general(a, b, (((1,), (1,)), ((), ())), preferred_element_type=F32)


def mm_tn(a, b):
    return lax.dot_general(a, b, (((0,), (0,)), ((), ())), preferred_element_type=F32)


def seq_layout(seq_lengths, tok_rows):
    seq_ends = jnp.cumsum(seq_lengths, dtype=jnp.int32)
    seq_starts = seq_ends - seq_lengths
    places = jnp.arange(tok_rows, dtype=jnp.int32)
    segment = jnp.sum(
        (places[:, None] >= seq_ends[None, :]).astype(jnp.int32), axis=1, dtype=jnp.int32
    )
    slot_match = segment[:, None] == jnp.arange(seq_lengths.shape[0], dtype=jnp.int32)[None, :]
    begins = jnp.sum(jnp.where(slot_match, seq_starts[None, :], 0), axis=1, dtype=jnp.int32)
    return (segment, places - begins)


def turn_columns(weights):
    rows, columns = weights.shape
    split = weights.reshape(rows, columns // HEAD, 2, HEAD // 2)
    return jnp.stack([-split[:, :, 1], split[:, :, 0]], axis=2).reshape(rows, columns)


def turn_matrix(columns):
    half = HEAD // 2
    turn = np.zeros((columns, columns), np.float32)
    for first in range(0, columns, HEAD):
        for i in range(half):
            turn[first + half + i, first + i] = 1.0
            turn[first + i, first + half + i] = -1.0
    return jnp.asarray(turn, BF)


def body(
    tokens,
    norm_attn,
    w_query,
    w_key,
    w_value,
    w_out,
    norm_moe,
    router,
    expert_gate,
    expert_up,
    expert_down,
    lengths,
    expert_ids,
    out_grad,
):
    highest = lax.Precision.HIGHEST
    ep_size = lax.axis_size("ep")
    tok_rows, width = tokens.shape
    q_cols, k_cols = w_query.shape[1], w_key.shape[1]
    kv = k_cols // HEAD
    group = q_cols // k_cols
    tp_size = lax.axis_size("tp")
    tp_at = lax.axis_index("tp")
    ep_at = lax.axis_index("ep")
    own = tok_rows // tp_size
    local_experts, _, ff = expert_gate.shape
    experts = router.shape[1]
    first = tp_at * own
    score_scale = HEAD ** (-0.5)

    def mine(array):
        return lax.dynamic_slice_in_dim(array, first, own, 0)

    def to_owners(parts):
        over_tp = lax.psum_scatter(parts, "tp", scatter_dimension=0, tiled=True)
        blocks = lax.all_to_all(
            over_tp.reshape(ep_size, own, parts.shape[1]), "ep", split_axis=0, concat_axis=0
        )
        return jnp.sum(blocks.astype(F32), axis=0)

    grad_own = mine(out_grad)
    grad_all = lax.all_gather(grad_own, BOTH, axis=0, tiled=True)
    ids_own = mine(expert_ids)
    mask_own = jnp.sum(
        (ids_own[:, :, None] == jnp.arange(experts, dtype=jnp.int32)[None, None, :]).astype(F32),
        axis=1,
    )

    w_gate_up = jnp.concatenate(
        [
            jnp.transpose(expert_gate, (1, 0, 2)).reshape(width, local_experts * ff),
            jnp.transpose(expert_up, (1, 0, 2)).reshape(width, local_experts * ff),
        ],
        axis=1,
    )
    w_down = expert_down.reshape(local_experts * ff, width)

    x_full = tokens.astype(F32)
    scale_one = lax.rsqrt(jnp.mean(x_full * x_full, axis=1, keepdims=True) + EPSILON)
    normed_one = (x_full * scale_one * norm_attn).astype(BF)
    segment, position = seq_layout(lengths[0], tok_rows)
    half = HEAD // 2
    inverse = ROPE_BASE ** (-2.0 * jnp.arange(half, dtype=F32) / HEAD)
    angles = position.astype(F32)[:, None] * inverse[None, :]
    cos_half, sin_half = jnp.cos(angles), jnp.sin(angles)
    cosine = jnp.concatenate([cos_half, cos_half] * (q_cols // HEAD), axis=1)
    sine = jnp.concatenate([sin_half, sin_half] * (q_cols // HEAD), axis=1)
    w_all = jnp.concatenate(
        [w_query, turn_columns(w_query), w_key, turn_columns(w_key), w_value], axis=1
    )
    projected = mm(normed_one, w_all)
    at = 2 * q_cols
    query_low = (projected[:, :q_cols] * cosine + projected[:, q_cols:at] * sine).astype(BF)
    key_low = (
        projected[:, at : at + k_cols] * cosine[:, :k_cols]
        + projected[:, at + k_cols : at + 2 * k_cols] * sine[:, :k_cols]
    ).astype(BF)
    value_flat = projected[:, at + 2 * k_cols :].astype(BF)

    def heads_q(array):
        return (
            array.reshape(tok_rows, kv, group, HEAD)
            .transpose(1, 2, 0, 3)
            .reshape(kv, group * tok_rows, HEAD)
        )

    def flat_q(array):
        return (
            array.reshape(kv, group, tok_rows, HEAD)
            .transpose(2, 0, 1, 3)
            .reshape(tok_rows, q_cols)
        )

    def heads_k(array):
        return array.reshape(tok_rows, kv, HEAD).transpose(1, 0, 2)

    def flat_k(array):
        return array.transpose(1, 0, 2).reshape(tok_rows, k_cols)

    query, key, value = heads_q(query_low), heads_k(key_low), heads_k(value_flat)
    place = jnp.arange(tok_rows, dtype=jnp.int32)
    allowed = (segment[:, None] == segment[None, :]) & (place[None, :] <= place[:, None])
    allowed = jnp.concatenate([allowed] * group, axis=0)
    scores = jnp.einsum("kbh,knh->kbn", query, key, preferred_element_type=F32) * score_scale
    scores = jnp.where(allowed[None], scores, -1e30)
    row_max = jnp.max(scores, axis=-1, keepdims=True)
    exp_terms = jnp.exp(scores - row_max)
    probs_full = exp_terms / jnp.sum(exp_terms, axis=-1, keepdims=True)
    prob_low = probs_full.astype(BF)
    mixed = jnp.einsum("kbn,knh->kbh", prob_low, value, preferred_element_type=F32)
    attended = flat_q(mixed.astype(BF))
    attn_partial = mm(attended, w_out)
    x_own = mine(tokens).astype(F32)
    attn_partial, grad_all = lax.optimization_barrier((attn_partial.astype(BF), grad_all))
    attn_sum = lax.psum_scatter(attn_partial, "tp", scatter_dimension=0, tiled=True)
    residual = x_own + attn_sum.astype(F32)
    scale_two = lax.rsqrt(jnp.mean(residual * residual, axis=1, keepdims=True) + EPSILON)
    normed_two = (residual * scale_two * norm_moe).astype(BF)

    logits = mm(normed_two, router)
    keep = mask_own > 0
    largest = jnp.max(jnp.where(keep, logits, -jnp.inf), axis=1, keepdims=True)
    own_exp = jnp.where(keep, jnp.exp(logits - largest), 0.0)
    gates_own = own_exp / jnp.sum(own_exp, axis=1, keepdims=True)
    gates_high = gates_own.astype(BF)
    gates_rest = (gates_own - gates_high.astype(F32)).astype(BF)

    lanes = -(-2 * experts // 128) * 128
    sent = jnp.concatenate(
        [normed_two, gates_high, gates_rest, jnp.zeros((own, lanes - 2 * experts), BF)], axis=1
    )
    sent_all = lax.all_gather(sent, BOTH, axis=0, tiled=True)
    rows_all = sent_all[:, :width]
    gates_all = sent_all[:, width:].astype(F32)
    gates = lax.dynamic_slice_in_dim(
        gates_all, ep_at * local_experts, local_experts, 1
    ) + lax.dynamic_slice_in_dim(gates_all, experts + ep_at * local_experts, local_experts, 1)
    all_rows = rows_all.shape[0]
    wide = local_experts * ff
    gate_wide = jnp.concatenate(
        [jnp.broadcast_to(gates[:, e : e + 1], (all_rows, ff)) for e in range(local_experts)],
        axis=1,
    )
    pre = mm(rows_all, w_gate_up)
    gate_pre, up_pre = pre[:, :wide], pre[:, wide:]
    grad_act = mm_nt(grad_all, w_down)
    sig = jax.nn.sigmoid(gate_pre)
    active = gate_pre * sig * up_pre
    grad_gates_wide = active * grad_act
    grad_gates_part = jnp.concatenate(
        [
            jnp.sum(grad_gates_wide[:, e * ff : (e + 1) * ff], axis=1, keepdims=True)
            for e in range(local_experts)
        ],
        axis=1,
    )
    weighted = (gate_wide * active).astype(BF)
    scaled_grad = gate_wide * grad_act
    grad_pre = jnp.concatenate(
        [
            (scaled_grad * up_pre * sig * (1.0 + gate_pre * (1.0 - sig))).astype(BF),
            (scaled_grad * gate_pre * sig).astype(BF),
        ],
        axis=1,
    )
    gates_dense = lax.dynamic_update_slice_in_dim(
        jnp.zeros((all_rows, lanes), BF),
        grad_gates_part.astype(BF),
        ep_at * local_experts,
        1,
    )
    row_part = jnp.concatenate([mm_nt(grad_pre, w_gate_up).astype(BF), gates_dense], axis=1)
    row_sums = to_owners(row_part)
    row_grads = row_sums[:, :width]
    grad_gates = row_sums[:, width : width + experts]
    mix_part = mm(weighted, w_down).astype(BF)
    grad_w_gu = mm_tn(rows_all, grad_pre)
    grad_w_gu = grad_w_gu.reshape(width, 2, local_experts, ff)
    grad_expert_gate = grad_w_gu[:, 0].transpose(1, 0, 2)
    grad_expert_up = grad_w_gu[:, 1].transpose(1, 0, 2)
    grad_expert_down = mm_tn(weighted, grad_all).reshape(local_experts, ff, width)

    grad_logits = gates_own * (
        grad_gates - jnp.sum(gates_own * grad_gates, axis=1, keepdims=True)
    )
    grad_router_part = jnp.dot(grad_logits.T, normed_two.astype(F32), precision=highest)
    router_input = jnp.dot(grad_logits, router.astype(F32).T, precision=highest)
    grad_normed_two = row_grads + router_input
    weighted_two = grad_normed_two * norm_moe
    grad_norm_moe = jnp.sum(grad_normed_two * residual * scale_two, axis=0)
    grad_residual = (
        grad_own.astype(F32)
        + scale_two * weighted_two
        - residual * scale_two**3 * jnp.mean(weighted_two * residual, axis=1, keepdims=True)
    )
    below = -(-(experts + 1) // 16) * 16
    sent_attn = jnp.concatenate(
        [
            grad_residual.astype(BF),
            grad_router_part.astype(BF),
            grad_norm_moe[None].astype(BF),
            jnp.zeros((below - experts - 1, width), BF),
        ],
        axis=0,
    )
    gathered = lax.all_gather(sent_attn, "tp", axis=0, tiled=False)
    grad_attn = gathered[:, :own].reshape(tok_rows, width)
    small = jnp.sum(gathered[:, own:].astype(F32), axis=0)
    mix_part, grad_attn = lax.optimization_barrier((mix_part, grad_attn))
    mixture = to_owners(mix_part)
    output_own = (residual + mixture).astype(BF)
    grad_w_out = mm_tn(attended, grad_attn)

    grad_attended = heads_q(mm_nt(grad_attn, w_out).astype(BF))
    grad_prob = jnp.einsum("kbh,knh->kbn", grad_attended, value, preferred_element_type=F32)
    row_inner = jnp.sum(probs_full * grad_prob, axis=-1, keepdims=True)
    grad_scores = (probs_full * (grad_prob - row_inner)).astype(BF)
    grad_q = flat_q(jnp.einsum("kbn,knh->kbh", grad_scores, key, preferred_element_type=F32))
    grad_k = flat_k(jnp.einsum("kbn,kbh->knh", grad_scores, query, preferred_element_type=F32))
    grad_v = flat_k(jnp.einsum("kbn,kbh->knh", prob_low, grad_attended, preferred_element_type=F32))
    grad_q = grad_q * score_scale
    grad_k = grad_k * score_scale
    turn = turn_matrix(q_cols)
    grad_q_low = (grad_q * cosine + mm((grad_q * sine).astype(BF), turn)).astype(BF)
    grad_k_low = (
        grad_k * cosine[:, :k_cols]
        + mm((grad_k * sine[:, :k_cols]).astype(BF), turn[:k_cols, :k_cols])
    ).astype(BF)
    grad_qkv = jnp.concatenate([grad_q_low, grad_k_low, grad_v.astype(BF)], axis=1)
    w_qkv = jnp.concatenate([w_query, w_key, w_value], axis=1)
    input_part = mm_nt(grad_qkv, w_qkv)
    norm_part = jnp.sum(input_part * x_full * scale_one, axis=0, keepdims=True)
    extra = jnp.concatenate([norm_part.astype(BF), jnp.zeros((15, width), BF)], axis=0)
    input_sent = jnp.concatenate(
        [
            input_part.astype(BF).reshape(tp_size, own, width),
            jnp.broadcast_to(extra[None], (tp_size, 16, width)),
        ],
        axis=1,
    )
    input_sums = lax.psum_scatter(
        input_sent.reshape(tp_size * (own + 16), width), "tp", scatter_dimension=0, tiled=True
    )
    grad_normed_one = input_sums[:own].astype(F32)
    grad_norm_attn = input_sums[own:]
    scale_own = mine(scale_one)
    weighted_one = grad_normed_one * norm_attn
    tokens_own = (
        grad_residual
        + scale_own * weighted_one
        - x_own * scale_own**3 * jnp.mean(weighted_one * x_own, axis=1, keepdims=True)
    )
    both = lax.all_gather(
        jnp.concatenate([output_own, tokens_own.astype(BF)], axis=0), "tp", axis=0, tiled=False
    )
    output = both[:, :own].reshape(tok_rows, width)
    grad_tokens = both[:, own:].reshape(tok_rows, width)
    stacked = jnp.concatenate(
        [grad_w_out.astype(BF), small.astype(BF), grad_norm_attn], axis=0
    )
    stacked = lax.psum(stacked, "ep").astype(F32)
    grad_w_out = stacked[: w_out.shape[0]]
    small = stacked[w_out.shape[0] : w_out.shape[0] + below]
    grad_norm_attn = stacked[w_out.shape[0] + below]
    grad_w_qkv = lax.psum(mm_tn(normed_one, grad_qkv).astype(BF), "ep").astype(F32)
    return (
        output,
        grad_tokens,
        grad_norm_attn,
        grad_w_qkv[:, :q_cols],
        grad_w_qkv[:, q_cols : q_cols + k_cols],
        grad_w_qkv[:, q_cols + k_cols :],
        grad_w_out,
        small[experts],
        small[:experts].T,
        grad_expert_gate,
        grad_expert_up,
        grad_expert_down,
    )


def solution(mesh):
    in_specs = (
        P("ep", None),
        P(),
        P(None, "tp"),
        P(None, "tp"),
        P(None, "tp"),
        P("tp", None),
        P(),
        P(),
        P("ep", None, "tp"),
        P("ep", None, "tp"),
        P("ep", "tp", None),
        P("ep", None),
        P("ep", None),
        P("ep", None),
    )
    out_specs = (
        P("ep", None),
        P("ep", None),
        P(),
        P(None, "tp"),
        P(None, "tp"),
        P(None, "tp"),
        P("tp", None),
        P(),
        P(),
        P("ep", None, "tp"),
        P("ep", None, "tp"),
        P("ep", "tp", None),
    )
    return jax.shard_map(body, mesh=mesh, in_specs=in_specs, out_specs=out_specs, check_vma=False)
```
